256 devices in a mesh: row: 32 (over y, z), col: 2 (over core), depth: 4 (over x).
Axes of the slice: x: 4, y: 4, z: 8, core: 2. Of those that a mesh axis runs over, the one named last changes fastest.
Arguments:
- lower_prev: float32 [3, 1024, 4096], P(None, 'row', 'depth'), may hold values from -0.09375 to 0.09375
- inner_blocks: float32 [3, 1024, 1024], P(None, 'row', 'depth'), may hold values from -0.1875 to 0.1875
- diag_inverse: float32 [3, 1024, 1024], P(None, 'depth'), as said below
- known_rows: float32 [4096, 2048], P('depth', 'col'), may hold values from -6 to 6
- right_sides: float32 [3, 1024, 2048], P(None, 'row', 'col'), may hold values from -6 to 6
Outputs:
- solved: float32 [3, 1024, 2048], P(None, 'depth', 'col')
The draws below stay inside these ranges and needn't reach their ends.
Inputs may be any that keep to these rules, and one draw needn't show every extreme that they name: Each diag_inverse[k] is lower triangular with diagonal entries between 0.7 and 1.3; its entries below the diagonal are of order 0.02 (normal with spread 0.6/32).
All inputs are finite; a program needn't handle non-finite values.
Results may differ from the reference program's by a relative error of at most 0.0001.
Values sent between devices are 32-bit elements; how exact they have to be, the bound alone decides.
A program may use at most 64 MiB of HBM per device.

```python
import jax
import jax.numpy as jnp
from jax import lax

NB = 1024
RHS = 2048
PREV = 4096


def draw_diag_inverse(key, part):
    first_key = jax.random.fold_in(key, 11)
    second_key = jax.random.fold_in(key, 23)
    positions = jnp.arange(NB)
    below = positions[:, None] > positions[None, :]
    same = positions[:, None] == positions[None, :]
    off_diag = jax.random.normal(first_key, (3, NB, NB), jnp.float32) * (0.6 / NB ** 0.5)
    diagonal = jax.random.uniform(second_key, (3, NB, 1), jnp.float32, 0.7, 1.3)
    return jnp.where(below, off_diag, 0.0) + jnp.where(same, diagonal, 0.0)


def levels(own_key, extent, split, least, top_value):
    def one(axis_at, blocks):
        steps = jax.random.uniform(jax.random.fold_in(jax.random.fold_in(own_key, 6), axis_at), (blocks,), jnp.float32, least / len(split), top_value / len(split))
        return jnp.repeat(jnp.exp(steps), extent[axis_at] // blocks).reshape((-1,) + (1,) * (len(extent) - axis_at - 1))

    level = one(*split[0])
    for cut in split[1:]:
        level = level * one(*cut)
    return level


def normal_values(rng, extent, spread, most, pieces=(), dtype=jnp.bfloat16):
    loudness = levels(rng, extent, pieces, -0.22, 0.18) if pieces else 1.0
    result = jax.random.normal(rng, extent, jnp.float32) * spread * loudness
    return jnp.minimum(jnp.maximum(result, -most), most).astype(dtype)


def setup_inputs(seed: int = 0) -> dict:
    keys = jax.random.split(jax.random.key(seed), 6)
    lower_prev = normal_values(keys[0], (3, NB, PREV), PREV ** -0.5, 0.09375, ((1, 32), (2, 4)), jnp.float32)
    inner_blocks = normal_values(keys[1], (3, NB, NB), NB ** -0.5, 0.1875, ((1, 32), (2, 4)), jnp.float32)
    diag_inverse = draw_diag_inverse(jax.random.fold_in(keys[5], 71), 0)
    known_rows = normal_values(keys[3], (PREV, RHS), 1.0, 6.0, ((0, 4), (1, 2)), jnp.float32)
    right_sides = normal_values(keys[4], (3, NB, RHS), 1.0, 6.0, ((1, 32), (2, 2)), jnp.float32)
    return {"lower_prev": lower_prev, "inner_blocks": inner_blocks, "diag_inverse": diag_inverse, "known_rows": known_rows, "right_sides": right_sides}


def reference(lower_prev, inner_blocks, diag_inverse, known_rows, right_sides):
    highest = lax.Precision.HIGHEST
    earlier_map = [[], [(0, 0)], [(0, 1), (1, 2)]]
    solved = []
    for section in range(3):
        update = jnp.dot(lower_prev[section], known_rows, precision=highest, preferred_element_type=jnp.float32)
        for earlier, which in earlier_map[section]:
            update = update + jnp.dot(inner_blocks[which], solved[earlier], precision=highest, preferred_element_type=jnp.float32)
        reduced = right_sides[section] - update
        solved.append(jnp.dot(diag_inverse[section], reduced, precision=highest, preferred_element_type=jnp.float32))
    return jnp.stack(solved)
```

```python
import functools

import jax
import jax.numpy as jnp
from jax import lax
from jax.experimental import pallas as pl
from jax.experimental.pallas import tpu as pltpu
from jax.sharding import PartitionSpec as P

MESH = pl.DeviceIdType.MESH
T = 8
LANES = 128


def split(value):
    high = value.astype(jnp.bfloat16)
    low = (value - high.astype(jnp.float32)).astype(jnp.bfloat16)
    return high, low


def dot(a, b):
    return jnp.dot(a, b, preferred_element_type=jnp.float32)


def three_pass(a_high, a_low, b):
    b_high, b_low = split(b)
    width = b.shape[1]
    both = dot(a_high, jnp.concatenate([b_high, b_low], axis=1))
    return both[:, :width] + (both[:, width:] + dot(a_low, b_high))


def wait_bytes(ref, sem):
    pltpu.make_async_copy(ref, ref, sem).wait()


def kernel(
    sizes,
    lower_hbm, inner_hbm, inverse_hbm, known_hbm, right_hbm,
    out_ref,
    lower_v, known_v, inverse_v, inverse_high, inverse_low, right_v, inner_v,
    p_send, p_recv, acc_v, red_v, count_v, u_send, u_recv, s_v,
    in_sem, known_sem,
    p_ssem, p_rsem, l_ssem, l_rsem, u_ssem, u_rsem, g_ssem, g_rsem,
    a_ssem, a_rsem, b_ssem, b_rsem,
):
    X, Y, Z = sizes
    row = lax.axis_index("row")
    col = lax.axis_index("col")
    x = lax.axis_index("depth")
    y = row // Z
    z = row % Z
    plane = X * Z
    me = x * Z + z
    step_rows = X * Y * Z * T
    quarter = step_rows // X // Y
    n_chunks = known_sem.shape[0]
    width = Z * LANES // n_chunks

    def place(px, py, pz):
        return (py * Z + pz, col, px)

    def z_lanes(pz):
        return pl.ds(pl.multiple_of(pz * LANES, LANES), LANES)

    lower_in = pltpu.make_async_copy(lower_hbm, lower_v, in_sem.at[0])
    lower_in.start()
    known_in = []
    for n in range(n_chunks):
        cut = pl.ds(n * width, width)
        copy = pltpu.make_async_copy(known_hbm.at[:, cut], known_v.at[:, cut], known_sem.at[n])
        copy.start()
        known_in.append(copy)
    right_in = pltpu.make_async_copy(right_hbm, right_v, in_sem.at[1])
    right_in.start()
    inner_in = pltpu.make_async_copy(inner_hbm, inner_v.at[:, z], in_sem.at[2])
    inner_in.start()
    inverse_in = pltpu.make_async_copy(inverse_hbm, inverse_v, in_sem.at[3])
    inverse_in.start()

    barrier = pltpu.get_barrier_semaphore()

    def greet_xz(o, carry):
        there = lax.rem(me + o, plane)
        pl.semaphore_signal(
            barrier, inc=1, device_id=place(there // Z, y, there % Z), device_id_type=MESH
        )
        return carry

    lax.fori_loop(1, plane, greet_xz, 0)

    def greet_xy(o, carry):
        there = lax.rem(y + 1 + o // X, Y)
        pl.semaphore_signal(barrier, inc=1, device_id=place(o % X, there, z), device_id_type=MESH)
        return carry

    lax.fori_loop(0, (Y - 1) * X, greet_xy, 0)

    lower_in.wait()
    right_in.wait()
    rows = 3 * X * T
    lower_high, lower_low = split(lower_v[...].reshape(rows, lower_v.shape[2]))
    lower_both = jnp.concatenate([lower_high, lower_low], axis=0)
    for n in range(n_chunks):
        known_in[n].wait()
        k_high, k_low = split(known_v[:, n * width : (n + 1) * width])
        first = dot(lower_both, k_high)
        prod = first[:rows] + (first[rows:] + dot(lower_high, k_low))
        for k in range(3):
            for xd in range(X):
                base = (k * X + xd) * T
                mine = right_v[k, xd * T : (xd + 1) * T, n * width : (n + 1) * width]
                value = jnp.where(x == xd, mine, 0.0) - prod[base : base + T]
                for zz in range(width // LANES):
                    zd = n * (width // LANES) + zz
                    p_send[k, xd * Z + zd] = value[:, zz * LANES : (zz + 1) * LANES]
    inner_in.wait()
    pl.semaphore_wait(barrier, plane - 1 + (Y - 1) * X)

    def send_p(first, count, slot):
        def body(o, carry):
            there = lax.rem(me + o, plane)
            pltpu.make_async_remote_copy(
                p_send.at[pl.ds(first, count), there],
                p_recv.at[pl.ds(first, count), me],
                p_ssem.at[slot],
                p_rsem.at[slot],
                device_id=place(there // Z, y, there % Z),
                device_id_type=MESH,
            ).start()
            return carry

        lax.fori_loop(1, plane, body, 0)

    def send_inner(which):
        def body(o, carry):
            pltpu.make_async_remote_copy(
                inner_v.at[which, z],
                inner_v.at[which, z],
                l_ssem.at[which],
                l_rsem.at[which],
                device_id=place(x, y, lax.rem(z + o, Z)),
                device_id_type=MESH,
            ).start()
            return carry

        lax.fori_loop(1, Z, body, 0)

    send_p(0, 1, 0)
    send_inner(0)
    send_p(1, 2, 1)
    send_inner(1)
    send_inner(2)
    for k in range(3):
        p_recv[k, me] = p_send[k, me]

    def p_sum(k):
        total = p_recv[k, 0:Z]
        for xs in range(1, X):
            total = total + p_recv[k, xs * Z : (xs + 1) * Z]
        return total

    def gather(k, value):
        acc_v[k] = value
        red_v[k, y, :, x] = value

        def body(o, carry):
            there = lax.rem(y * X + x + o, X * Y)
            pltpu.make_async_remote_copy(
                acc_v.at[k],
                red_v.at[k, y, :, x],
                g_ssem.at[k],
                g_rsem.at[k],
                device_id=place(there % X, there // X, z),
                device_id_type=MESH,
            ).start()
            return carry

        lax.fori_loop(1, X * Y, body, 0)

    def solve(k):
        wait_bytes(count_v.at[pl.ds(0, X * Y - 1)], g_rsem.at[k])
        value = three_pass(
            inverse_high[k], inverse_low[k], red_v[k].reshape(step_rows, LANES)
        )
        s_v[k] = value
        out_ref[k, :, z_lanes(z)] = value

    def apply_inner(which, k):
        high, low = split(inner_v[which].reshape(Z * X * T, inner_v.shape[3]))
        return three_pass(high, low, s_v[k]).reshape(Z, X, T, LANES)

    def send_update(j, value):
        for xd in range(X):
            u_send[j, xd] = value[:, xd]
        u_recv[j, x] = u_send[j, x]

        def body(o, carry):
            there = lax.rem(x + o, X)
            pltpu.make_async_remote_copy(
                u_send.at[j, there],
                u_recv.at[j, x],
                u_ssem.at[j],
                u_rsem.at[j],
                device_id=place(there, y, z),
                device_id_type=MESH,
            ).start()
            return carry

        lax.fori_loop(1, X, body, 0)

    def update_sum(j):
        wait_bytes(u_recv.at[j, pl.ds(0, X - 1)], u_rsem.at[j])
        total = u_recv[j, 0]
        for xs in range(1, X):
            total = total + u_recv[j, xs]
        return total

    own_rows = pl.ds(pl.multiple_of(y * quarter, T), quarter)

    def spread_z(k):
        def body(o, carry):
            pltpu.make_async_remote_copy(
                s_v.at[k, own_rows],
                out_ref.at[k, own_rows, z_lanes(z)],
                a_ssem.at[k],
                a_rsem.at[k, o],
                device_id=place(x, y, lax.rem(z + o, Z)),
                device_id_type=MESH,
            ).start()
            return carry

        lax.fori_loop(1, Z, body, 0)

    def spread_y(k):
        def body(o, carry):
            block = out_ref.at[k, own_rows, z_lanes(lax.rem(z + Z - o, Z))]
            wait_bytes(block, a_rsem.at[k, o])
            for p in range(1, Y):
                pltpu.make_async_remote_copy(
                    block,
                    block,
                    b_ssem.at[k],
                    b_rsem.at[k],
                    device_id=place(x, lax.rem(y + p, Y), z),
                    device_id_type=MESH,
                ).start()
            return carry

        lax.fori_loop(1, Z, body, 0)

    wait_bytes(p_recv.at[pl.ds(0, 1), pl.ds(0, plane - 1)], p_rsem.at[0])
    gather(0, p_sum(0))
    inverse_in.wait()
    for k in range(3):
        high, low = split(inverse_v[k])
        inverse_high[k] = high
        inverse_low[k] = low
    solve(0)

    wait_bytes(inner_v.at[0, pl.ds(0, Z - 1)], l_rsem.at[0])
    send_update(0, apply_inner(0, 0))
    spread_z(0)
    wait_bytes(p_recv.at[pl.ds(1, 2), pl.ds(0, plane - 1)], p_rsem.at[1])
    wait_bytes(inner_v.at[1, pl.ds(0, Z - 1)], l_rsem.at[1])
    early = apply_inner(1, 0)
    gather(1, p_sum(1) - update_sum(0))
    spread_y(0)
    wait_bytes(inner_v.at[2, pl.ds(0, Z - 1)], l_rsem.at[2])
    solve(1)

    send_update(1, early + apply_inner(2, 1))
    spread_z(1)
    gather(2, p_sum(2) - update_sum(1))
    spread_y(1)
    solve(2)
    spread_z(2)
    spread_y(2)

    wait_bytes(p_send.at[pl.ds(0, 1), pl.ds(0, plane - 1)], p_ssem.at[0])
    wait_bytes(p_send.at[pl.ds(1, 2), pl.ds(0, plane - 1)], p_ssem.at[1])
    for k in range(3):
        wait_bytes(inner_v.at[k, pl.ds(0, Z - 1)], l_ssem.at[k])
        wait_bytes(count_v.at[pl.ds(0, X * Y - 1)], g_ssem.at[k])
        wait_bytes(out_ref.at[k, pl.ds(0, quarter), pl.ds(0, (Z - 1) * LANES)], a_ssem.at[k])
        forwarded = out_ref.at[k, pl.ds(0, (Y - 1) * quarter), pl.ds(0, (Z - 1) * LANES)]
        wait_bytes(forwarded, b_ssem.at[k])
        wait_bytes(forwarded, b_rsem.at[k])
    for j in range(2):
        wait_bytes(u_send.at[j, pl.ds(0, X - 1)], u_ssem.at[j])


def on_device(sizes, lower_prev, inner_blocks, diag_inverse, known_rows, right_sides):
    X, Y, Z = sizes
    step_rows = X * Y * Z * T
    f32 = jnp.float32
    dma = pltpu.SemaphoreType.DMA
    return pl.pallas_call(
        functools.partial(kernel, sizes),
        out_shape=jax.ShapeDtypeStruct((3, step_rows // X, Z * LANES), f32),
        in_specs=[pl.BlockSpec(memory_space=pl.ANY)] * 5,
        out_specs=pl.BlockSpec(memory_space=pltpu.VMEM),
        scratch_shapes=[
            pltpu.VMEM(lower_prev.shape, f32),
            pltpu.VMEM(known_rows.shape, f32),
            pltpu.VMEM(diag_inverse.shape, f32),
            pltpu.VMEM(diag_inverse.shape, jnp.bfloat16),
            pltpu.VMEM(diag_inverse.shape, jnp.bfloat16),
            pltpu.VMEM(right_sides.shape, f32),
            pltpu.VMEM((3, Z) + inner_blocks.shape[1:], f32),
            pltpu.VMEM((3, X * Z, T, LANES), f32),
            pltpu.VMEM((3, X * Z, T, LANES), f32),
            pltpu.VMEM((3, Z, T, LANES), f32),
            pltpu.VMEM((3, Y, Z, X, T, LANES), f32),
            pltpu.VMEM((X * Y, Z, T, LANES), f32),
            pltpu.VMEM((2, X, Z, T, LANES), f32),
            pltpu.VMEM((2, X, Z, T, LANES), f32),
            pltpu.VMEM((3, step_rows // X, LANES), f32),
            dma((4,)),
            dma((max(1, Z // 2),)),
            dma((2,)), dma((2,)),
            dma((3,)), dma((3,)),
            dma((2,)), dma((2,)),
            dma((3,)), dma((3,)),
            dma((3,)), dma((3, Z)),
            dma((3,)), dma((3,)),
        ],
        compiler_params=pltpu.CompilerParams(
            collective_id=0, has_side_effects=True, vmem_limit_bytes=56 * 1024 * 1024
        ),
    )(lower_prev, inner_blocks, diag_inverse, known_rows, right_sides)


def solution(mesh):
    X = mesh.shape["depth"]
    Y = 4 if mesh.shape["row"] == 32 else 2
    sizes = (X, Y, mesh.shape["row"] // Y)
    placed = (
        P(None, "row", "depth"),
        P(None, "row", "depth"),
        P(None, "depth", None),
        P("depth", "col"),
        P(None, "row", "col"),
    )
    return jax.shard_map(
        functools.partial(on_device, sizes),
        mesh=mesh,
        in_specs=placed,
        out_specs=P(None, "depth", "col"),
        check_vma=False,
    )
```

```python
import functools

import jax
import jax.numpy as jnp
from jax import lax
from jax.experimental import pallas as pl
from jax.experimental.pallas import tpu as pltpu
from jax.sharding import PartitionSpec as P

MESH = pl.DeviceIdType.MESH
T = 8
LANES = 128


def split(value):
    high = value.astype(jnp.bfloat16)
    low = (value - high.astype(jnp.float32)).astype(jnp.bfloat16)
    return high, low


def dot(a, b):
    return jnp.dot(a, b, preferred_element_type=jnp.float32)


def three_pass(a_high, a_low, b):
    b_high, b_low = split(b)
    width = b.shape[1]
    both = dot(a_high, jnp.concatenate([b_high, b_low], axis=1))
    return both[:, :width] + (both[:, width:] + dot(a_low, b_high))


def wait_bytes(ref, sem):
    pltpu.make_async_copy(ref, ref, sem).wait()


def kernel(
    sizes,
    lower_hbm, inner_hbm, inverse_hbm, known_hbm, right_hbm,
    out_ref,
    lower_v, known_v, inverse_v, inverse_high, inverse_low, right_v, inner_v,
    p_send, p_recv, q_send, q_recv, acc_v, red_v, u_send, u_recv,
    in_sem, known_sem,
    p_ssem, p_rsem, q_ssem, q_rsem, l_ssem, l_rsem, u_ssem, u_rsem, g_ssem, g_rsem,
    r_ssem, r_rsem, a_ssem, a_rsem, b_ssem, b_rsem,
):
    X, Y, Z = sizes
    row = lax.axis_index("row")
    col = lax.axis_index("col")
    x = lax.axis_index("depth")
    y = row // Z
    z = row % Z
    step_rows = X * Y * Z * T
    own = step_rows // X
    quarter = own // Y
    n_chunks = known_sem.shape[0]
    width = Z * LANES // n_chunks

    def on_x(o):
        return (row, col, lax.rem(x + o, X))

    def on_y(o):
        return (lax.rem(y + o, Y) * Z + z, col, x)

    def on_z(o):
        return (y * Z + lax.rem(z + o, Z), col, x)

    def z_lanes(pz):
        return pl.ds(pl.multiple_of(pz * LANES, LANES), LANES)

    def send(src, dst, ssem, rsem, device):
        pltpu.make_async_remote_copy(
            src, dst, ssem, rsem, device_id=device, device_id_type=MESH
        ).start()

    lower_in = pltpu.make_async_copy(lower_hbm, lower_v, in_sem.at[0])
    lower_in.start()
    known_in = []
    for n in range(n_chunks):
        cut = pl.ds(n * width, width)
        copy = pltpu.make_async_copy(known_hbm.at[:, cut], known_v.at[:, cut], known_sem.at[n])
        copy.start()
        known_in.append(copy)
    right_in = pltpu.make_async_copy(right_hbm, right_v, in_sem.at[1])
    right_in.start()
    inner_in = pltpu.make_async_copy(inner_hbm, inner_v.at[:, z], in_sem.at[2])
    inner_in.start()
    inverse_in = pltpu.make_async_copy(inverse_hbm, inverse_v, in_sem.at[3])
    inverse_in.start()

    red_v[...] = jnp.zeros_like(red_v)

    barrier = pltpu.get_barrier_semaphore()
    for on, extent in ((on_x, X), (on_z, Z), (on_y, Y)):
        for o in range(1, extent):
            pl.semaphore_signal(barrier, inc=1, device_id=on(o), device_id_type=MESH)

    lower_in.wait()
    right_in.wait()
    rows = 3 * X * T
    lower_high, lower_low = split(lower_v[...].reshape(rows, lower_v.shape[2]))
    lower_both = jnp.concatenate([lower_high, lower_low], axis=0)
    for n in range(n_chunks):
        known_in[n].wait()
        cut = slice(n * width, (n + 1) * width)
        k_high, k_low = split(known_v[:, cut])
        first = dot(lower_both, k_high)
        prod = first[:rows] + (first[rows:] + dot(lower_high, k_low))
        for k in range(3):
            for xd in range(X):
                base = (k * X + xd) * T
                mine = right_v[k, xd * T : (xd + 1) * T, cut]
                p_send[k, xd, :, cut] = jnp.where(x == xd, mine, 0.0) - prod[base : base + T]
    pl.semaphore_wait(barrier, X - 1 + Y - 1 + Z - 1)

    steps = (pl.ds(0, 1), pl.ds(1, 2))

    def p_to_x(slot):
        for o in range(1, X):
            there = lax.rem(x + o, X)
            send(
                p_send.at[steps[slot], there], p_recv.at[steps[slot], o],
                p_ssem.at[slot], p_rsem.at[slot], on_x(o),
            )

    def p_to_z(slot):
        wait_bytes(p_recv.at[steps[slot], pl.ds(1, X - 1)], p_rsem.at[slot])
        for k in ((0,), (1, 2))[slot]:
            total = p_send[k, x]
            for o in range(1, X):
                total = total + p_recv[k, o]
            for zd in range(Z):
                q_send[k, zd] = total[:, zd * LANES : (zd + 1) * LANES]
            q_recv[k, z] = q_send[k, z]
        for o in range(1, Z):
            there = lax.rem(z + o, Z)
            send(
                q_send.at[steps[slot], there], q_recv.at[steps[slot], z],
                q_ssem.at[slot], q_rsem.at[slot], on_z(o),
            )

    def q_wait(slot):
        wait_bytes(q_recv.at[steps[slot], pl.ds(0, Z - 1)], q_rsem.at[slot])

    def inner_to_z(slot):
        for o in range(1, Z):
            block = inner_v.at[steps[slot], z]
            send(block, block, l_ssem.at[slot], l_rsem.at[slot], on_z(o))

    def inner_wait(slot):
        wait_bytes(inner_v.at[steps[slot], pl.ds(0, Z - 1)], l_rsem.at[slot])

    def split_inverse(k):
        high, low = split(inverse_v[k])
        inverse_high[k] = high
        inverse_low[k] = low

    places = X * Y
    here = y * X + x

    def gather(k, value):
        acc_v[k] = value
        red_v[k, y, :, x] = value

        def body(o, carry):
            there = lax.rem(here + o, places)

            @pl.when(there % X >= y)
            def _():
                send(
                    acc_v.at[k], red_v.at[k, y, :, x],
                    g_ssem.at[k, o], g_rsem.at[k, here],
                    ((there // X) * Z + z, col, there % X),
                )

            return carry

        lax.fori_loop(1, places, body, 0)

    def gather_wait(k):
        def body(source, carry):
            @pl.when((source // X <= x) & (source != here))
            def _():
                wait_bytes(red_v.at[k, source // X, :, source % X], g_rsem.at[k, source])

            return carry

        lax.fori_loop(0, places, body, 0)

    def gather_done(k):
        def body(o, carry):
            @pl.when(lax.rem(here + o, places) % X >= y)
            def _():
                wait_bytes(acc_v.at[k], g_ssem.at[k, o])

            return carry

        lax.fori_loop(1, places, body, 0)

    def solve(k):
        gather_wait(k)
        value = three_pass(
            inverse_high[k], inverse_low[k], red_v[k].reshape(step_rows, LANES)
        )
        out_ref[k, :, z_lanes(z)] = value
        return value

    def apply_inner(which, value):
        high, low = split(inner_v[which].reshape(Z * X * T, inner_v.shape[3]))
        return three_pass(high, low, value).reshape(Z, X, T, LANES)

    def update_to_x(j, value):
        for xd in range(X):
            u_send[j, xd] = value[:, xd]
        for o in range(1, X):
            there = lax.rem(x + o, X)
            send(u_send.at[j, there], u_recv.at[j, o], u_ssem.at[j], u_rsem.at[j], on_x(o))

    def update_sum(j):
        wait_bytes(u_recv.at[j, pl.ds(1, X - 1)], u_rsem.at[j])
        total = u_send[j, x]
        for o in range(1, X):
            total = total + u_recv[j, o]
        return total

    hops = Z // 2
    half = own // 2

    def ring_block(k, hop, way):
        lanes = z_lanes(lax.rem(z + (Z - hop if way == 0 else hop), Z))
        if hop == hops - 1:
            return out_ref.at[k, pl.ds(way * half, half), lanes]
        return out_ref.at[k, :, lanes]

    def ring_wait(k, hop):
        for way in range(2):
            came = ring_block(k, hop, way)
            wait_bytes(came, r_rsem.at[k, hop, way])

    def ring(k, hop):
        if hop >= hops:
            return
        if hop > 0:
            ring_wait(k, hop - 1)
        for way in range(2):
            block = ring_block(k, hop, way)
            send(
                block, block, r_ssem.at[k, hop, way], r_rsem.at[k, hop, way],
                on_z(1 if way == 0 else Z - 1),
            )

    def ring_done(k):
        ring_wait(k, hops - 1)
        for hop in range(hops):
            for way in range(2):
                wait_bytes(ring_block(k, hop, way), r_ssem.at[k, hop, way])

    last = 2
    own_rows = pl.ds(pl.multiple_of(y * quarter, T), quarter)
    near = sorted(range(1, Z), key=lambda o: (min(o, Z - o), o))

    def spread_z():
        block = out_ref.at[last, own_rows, z_lanes(z)]
        for o in near:
            send(block, block, a_ssem.at[0], a_rsem.at[o], on_z(o))

    def spread_y(offsets):
        for o in offsets:
            block = out_ref.at[last, own_rows, z_lanes(lax.rem(z + Z - o, Z))]
            wait_bytes(block, a_rsem.at[o])
            for p in range(1, Y):
                send(block, block, b_ssem.at[0], b_rsem.at[0], on_y(p))

    p_to_x(0)
    p_to_x(1)
    inner_in.wait()
    p_to_z(0)
    inner_to_z(0)
    p_to_z(1)
    inverse_in.wait()
    split_inverse(0)
    q_wait(0)
    gather(0, q_recv[0])
    inner_to_z(1)
    split_inverse(1)
    split_inverse(2)
    solved = solve(0)

    inner_wait(0)
    update_to_x(0, apply_inner(0, solved))
    ring(0, 0)
    q_wait(1)
    inner_wait(1)
    early = apply_inner(1, solved)
    gather(1, q_recv[1] - update_sum(0))
    ring(0, 1)
    solved = solve(1)

    update_to_x(1, early + apply_inner(2, solved))
    ring(1, 0)
    ring(0, 2)
    gather(2, q_recv[2] - update_sum(1))
    ring(1, 1)
    ring(0, 3)
    solve(2)
    spread_z()
    ring(1, 2)
    spread_y(near[:4])
    ring(1, 3)
    spread_y(near[4:])

    ring_done(0)
    ring_done(1)
    for slot in range(2):
        wait_bytes(p_send.at[steps[slot], pl.ds(0, X - 1)], p_ssem.at[slot])
        wait_bytes(q_send.at[steps[slot], pl.ds(0, Z - 1)], q_ssem.at[slot])
        wait_bytes(inner_v.at[steps[slot], pl.ds(0, Z - 1)], l_ssem.at[slot])
        wait_bytes(u_send.at[slot, pl.ds(0, X - 1)], u_ssem.at[slot])
    for k in range(3):
        gather_done(k)
    lanes = pl.ds(0, (Z - 1) * LANES)
    wait_bytes(out_ref.at[last, pl.ds(0, quarter), lanes], a_ssem.at[0])
    passed_on = out_ref.at[last, pl.ds(0, (Y - 1) * quarter), lanes]
    wait_bytes(passed_on, b_ssem.at[0])
    wait_bytes(passed_on, b_rsem.at[0])


def on_device(sizes, lower_prev, inner_blocks, diag_inverse, known_rows, right_sides):
    X, Y, Z = sizes
    step_rows = X * Y * Z * T
    f32 = jnp.float32
    dma = pltpu.SemaphoreType.DMA
    return pl.pallas_call(
        functools.partial(kernel, sizes),
        out_shape=pltpu.VMEM((3, step_rows // X, Z * LANES), f32),
        in_specs=[pl.BlockSpec(memory_space=pl.ANY)] * 5,
        out_specs=pl.BlockSpec(memory_space=pltpu.VMEM),
        scratch_shapes=[
            pltpu.VMEM(lower_prev.shape, f32),
            pltpu.VMEM(known_rows.shape, f32),
            pltpu.VMEM(diag_inverse.shape, f32),
            pltpu.VMEM(diag_inverse.shape, jnp.bfloat16),
            pltpu.VMEM(diag_inverse.shape, jnp.bfloat16),
            pltpu.VMEM(right_sides.shape, f32),
            pltpu.VMEM((3, Z) + inner_blocks.shape[1:], f32),
            pltpu.VMEM((3, X, T, Z * LANES), f32),
            pltpu.VMEM((3, X, T, Z * LANES), f32),
            pltpu.VMEM((3, Z, T, LANES), f32),
            pltpu.VMEM((3, Z, T, LANES), f32),
            pltpu.VMEM((3, Z, T, LANES), f32),
            pltpu.VMEM((3, Y, Z, X, T, LANES), f32),
            pltpu.VMEM((2, X, Z, T, LANES), f32),
            pltpu.VMEM((2, X, Z, T, LANES), f32),
            dma((4,)),
            dma((max(1, Z // 2),)),
            dma((2,)), dma((2,)),
            dma((2,)), dma((2,)),
            dma((2,)), dma((2,)),
            dma((2,)), dma((2,)),
            dma((3, X * Y)), dma((3, X * Y)),
            dma((2, Z // 2, 2)), dma((2, Z // 2, 2)),
            dma((1,)), dma((Z,)),
            dma((1,)), dma((1,)),
        ],
        compiler_params=pltpu.CompilerParams(
            collective_id=0, has_side_effects=True, vmem_limit_bytes=56 * 1024 * 1024
        ),
    )(lower_prev, inner_blocks, diag_inverse, known_rows, right_sides)


def solution(mesh):
    X = mesh.shape["depth"]
    Y = 4 if mesh.shape["row"] == 32 else 2
    sizes = (X, Y, mesh.shape["row"] // Y)
    placed = (
        P(None, "row", "depth"),
        P(None, "row", "depth"),
        P(None, "depth", None),
        P("depth", "col"),
        P(None, "row", "col"),
    )
    return jax.shard_map(
        functools.partial(on_device, sizes),
        mesh=mesh,
        in_specs=placed,
        out_specs=P(None, "depth", "col"),
        check_vma=False,
    )
```

```python
import functools

import jax
import jax.numpy as jnp
from jax import lax
from jax.experimental import pallas as pl
from jax.experimental.pallas import tpu as pltpu
from jax.sharding import PartitionSpec as P

MESH = pl.DeviceIdType.MESH
T = 8
LANES = 128


def split(value):
    high = value.astype(jnp.bfloat16)
    low = (value - high.astype(jnp.float32)).astype(jnp.bfloat16)
    return high, low


def dot(a, b):
    return jnp.dot(a, b, preferred_element_type=jnp.float32)


def three_pass(a_high, a_low, b):
    b_high, b_low = split(b)
    width = b.shape[1]
    both = dot(a_high, jnp.concatenate([b_high, b_low], axis=1))
    return both[:, :width] + (both[:, width:] + dot(a_low, b_high))


def wait_bytes(ref, sem):
    pltpu.make_async_copy(ref, ref, sem).wait()


def kernel(
    sizes,
    lower_hbm, inner_hbm, inverse_hbm, known_hbm, right_hbm,
    out_ref,
    lower_v, known_v, inverse_v, inverse_high, inverse_low, right_v, inner_v,
    first_send, first_recv, p_send, p_recv, q_send, q_recv, acc_v, red_v, u_send, u_recv,
    in_sem, known_sem,
    first_ssem, first_rsem, p_ssem, p_rsem, q_ssem, q_rsem, l_ssem, l_rsem, h_ssem, h_rsem, u_ssem, u_rsem, g_ssem, g_rsem,
    a_ssem, a_rsem, b_ssem, b_rsem,
):
    X, Y, Z = sizes
    reach = (1, 1, 2)
    row = lax.axis_index("row")
    col = lax.axis_index("col")
    x = lax.axis_index("depth")
    y = row // Z
    z = row % Z
    step_rows = X * Y * Z * T
    own = step_rows // X
    quarter = own // Y
    n_chunks = known_sem.shape[0]
    width = Z * LANES // n_chunks

    def on_x(o):
        return (row, col, lax.rem(x + o, X))

    def on_y(o):
        return (lax.rem(y + o, Y) * Z + z, col, x)

    def on_z(o):
        return (y * Z + lax.rem(z + o, Z), col, x)

    def z_lanes(pz):
        return pl.ds(pl.multiple_of(pz * LANES, LANES), LANES)

    def send(src, dst, ssem, rsem, device):
        pltpu.make_async_remote_copy(
            src, dst, ssem, rsem, device_id=device, device_id_type=MESH
        ).start()

    def far(o, extent):
        return min(o, extent - o)

    def far_first(extent):
        return sorted(range(1, extent), key=lambda o: -far(o, extent))

    xz = sorted(
        ((dx, dz) for dx in range(X) for dz in range(Z) if dx or dz),
        key=lambda d: -(far(d[0], X) + far(d[1], Z)),
    )
    xy = sorted(
        ((dx, dy) for dx in range(X) for dy in range(Y) if dx or dy),
        key=lambda d: -(far(d[0], X) + far(d[1], Y)),
    )

    barrier = pltpu.get_barrier_semaphore()
    for dx, dz in xz:
        device = (y * Z + lax.rem(z + dz, Z), col, lax.rem(x + dx, X))
        pl.semaphore_signal(barrier, inc=1, device_id=device, device_id_type=MESH)
    for o in range(1, Y):
        pl.semaphore_signal(barrier, inc=1, device_id=on_y(o), device_id_type=MESH)

    other_core = (row, 1 - col, x)
    pl.semaphore_signal(barrier, inc=1, device_id=other_core, device_id_type=MESH)

    lower_in = pltpu.make_async_copy(lower_hbm, lower_v, in_sem.at[0])
    lower_in.start()
    known_in = []
    for n in range(n_chunks):
        cut = pl.ds(n * width, width)
        copy = pltpu.make_async_copy(known_hbm.at[:, cut], known_v.at[:, cut], known_sem.at[n])
        copy.start()
        known_in.append(copy)
    right_in = pltpu.make_async_copy(right_hbm, right_v, in_sem.at[1])
    right_in.start()
    inner_in = pltpu.make_async_copy(inner_hbm, inner_v.at[:, 0], in_sem.at[2])
    inner_in.start()
    inverse_in = pltpu.make_async_copy(inverse_hbm, inverse_v, in_sem.at[3])
    inverse_in.start()

    for yy in range(1, Y):
        @pl.when(yy > x)
        def _():
            red_v[:, yy] = jnp.zeros_like(red_v[:, yy])

    lower_in.wait()
    right_in.wait()
    rows = 3 * X * T
    lower_high, lower_low = split(lower_v[...].reshape(rows, lower_v.shape[2]))
    lower_both = jnp.concatenate([lower_high, lower_low], axis=0)
    for n in range(n_chunks):
        known_in[n].wait()
        cut = slice(n * width, (n + 1) * width)
        k_high, k_low = split(known_v[:, cut])
        first = dot(lower_both, k_high)
        prod = first[:rows] + (first[rows:] + dot(lower_high, k_low))
        for k in range(3):
            for xd in range(X):
                base = (k * X + xd) * T
                mine = right_v[k, xd * T : (xd + 1) * T, cut]
                value = jnp.where(x == xd, mine, 0.0) - prod[base : base + T]
                if k > 0:
                    p_send[k - 1, xd, :, cut] = value
                else:
                    for zz in range(width // LANES):
                        zd = n * (width // LANES) + zz
                        first_send[xd * Z + zd] = value[:, zz * LANES : (zz + 1) * LANES]
    inverse_in.wait()
    for k in range(3):
        high, low = split(inverse_v[k])
        inverse_high[k] = high
        inverse_low[k] = low
    inner_in.wait()
    pl.semaphore_wait(barrier, len(xz) + Y)

    steps = (pl.ds(0, 1), pl.ds(1, 2))
    me = x * Z + z

    def first_to_xz():
        for dx, dz in xz:
            xd = lax.rem(x + dx, X)
            zd = lax.rem(z + dz, Z)
            send(
                first_send.at[xd * Z + zd], first_recv.at[me],
                first_ssem.at[0], first_rsem.at[0], (y * Z + zd, col, xd),
            )
        first_recv[me] = first_send[me]

    def first_sum():
        wait_bytes(first_recv.at[pl.ds(0, X * Z - 1)], first_rsem.at[0])
        total = first_recv[0:Z]
        for xs in range(1, X):
            total = total + first_recv[xs * Z : (xs + 1) * Z]
        return total

    def p_to_x():
        for o in far_first(X):
            there = lax.rem(x + o, X)
            send(p_send.at[:, there], p_recv.at[:, o], p_ssem.at[0], p_rsem.at[0], on_x(o))

    def p_to_z():
        wait_bytes(p_recv.at[:, pl.ds(1, X - 1)], p_rsem.at[0])
        for k in range(2):
            total = p_send[k, x]
            for o in range(1, X):
                total = total + p_recv[k, o]
            for zd in range(Z):
                q_send[k, zd] = total[:, zd * LANES : (zd + 1) * LANES]
            q_recv[k, z] = q_send[k, z]
        for o in far_first(Z):
            there = lax.rem(z + o, Z)
            send(q_send.at[:, there], q_recv.at[:, z], q_ssem.at[0], q_rsem.at[0], on_z(o))

    def q_wait():
        wait_bytes(q_recv.at[:, pl.ds(0, Z - 1)], q_rsem.at[0])

    half = X * T // 2
    my_half = pl.ds(pl.multiple_of(col * half, T), half)

    def inner_to_z(slot):
        for o in far_first(Z):
            send(
                inner_v.at[steps[slot], 0, my_half], inner_v.at[steps[slot], o, my_half],
                l_ssem.at[slot], l_rsem.at[slot], on_z(o),
            )

    def inner_to_core(slot):
        block = inner_v.at[steps[slot], pl.ds(1, Z - 1), my_half]
        wait_bytes(block, l_rsem.at[slot])
        send(block, block, h_ssem.at[slot], h_rsem.at[slot], other_core)

    def inner_wait(slot):
        wait_bytes(inner_v.at[steps[slot], pl.ds(1, Z - 1), my_half], h_rsem.at[slot])

    def gather(k, value):
        acc_v[k] = value
        red_v[k, y, :, x] = value
        for i, (dx, dy) in enumerate(xy):
            xd = lax.rem(x + dx, X)

            @pl.when(xd >= y)
            def _():
                send(
                    acc_v.at[k], red_v.at[k, y, :, x], g_ssem.at[k, i], g_rsem.at[k, i],
                    (lax.rem(y + dy, Y) * Z + z, col, xd),
                )

    def gather_wait(k):
        for i, (dx, dy) in enumerate(xy):
            ys = lax.rem(y + Y - dy, Y)

            @pl.when(ys <= x)
            def _():
                wait_bytes(red_v.at[k, ys, :, lax.rem(x + X - dx, X)], g_rsem.at[k, i])

    def gather_done(k):
        for i, (dx, dy) in enumerate(xy):

            @pl.when(lax.rem(x + dx, X) >= y)
            def _():
                wait_bytes(acc_v.at[k], g_ssem.at[k, i])

    def solve(k):
        gather_wait(k)
        value = three_pass(
            inverse_high[k], inverse_low[k], red_v[k].reshape(step_rows, LANES)
        )
        out_ref[k, :, z_lanes(z)] = value
        return value

    def apply_inner(which, value):
        high, low = split(inner_v[which].reshape(Z * X * T, inner_v.shape[3]))
        return three_pass(high, low, value).reshape(Z, X, T, LANES)

    def update_to_x(j, value):
        for o in range(Z):
            u_send[j, :, lax.rem(z + Z - o, Z)] = value[o]
        for o in far_first(X):
            there = lax.rem(x + o, X)
            send(u_send.at[j, there], u_recv.at[j, o], u_ssem.at[j], u_rsem.at[j], on_x(o))

    def update_sum(j):
        wait_bytes(u_recv.at[j, pl.ds(1, X - 1)], u_rsem.at[j])
        total = u_send[j, x]
        for o in range(1, X):
            total = total + u_recv[j, o]
        return total

    own_rows = pl.ds(pl.multiple_of(y * quarter, T), quarter)

    def spread_z(k, reach):
        block = out_ref.at[k, own_rows, z_lanes(z)]
        for o in far_first(Z):
            if far(o, Z) > reach:
                send(block, block, a_ssem.at[k, o], a_rsem.at[k, o], on_z(o))
        block = out_ref.at[k, :, z_lanes(z)]
        for o in far_first(Z)[::-1]:
            if far(o, Z) <= reach:
                send(block, block, a_ssem.at[k, o], a_rsem.at[k, o], on_z(o))

    def spread_y(k, reach):
        for o in far_first(Z)[::-1]:
            if far(o, Z) > reach:
                block = out_ref.at[k, own_rows, z_lanes(lax.rem(z + Z - o, Z))]
                wait_bytes(block, a_rsem.at[k, o])
                for p in far_first(Y):
                    send(block, block, b_ssem.at[k], b_rsem.at[k], on_y(p))

    def spread_done(k, reach):
        others = 0
        for o in range(1, Z):
            if far(o, Z) > reach:
                wait_bytes(out_ref.at[k, own_rows, z_lanes(z)], a_ssem.at[k, o])
                others += 1
            else:
                block = out_ref.at[k, :, z_lanes(z)]
                wait_bytes(block, a_ssem.at[k, o])
                wait_bytes(block, a_rsem.at[k, o])
        passed_on = out_ref.at[k, pl.ds(0, (Y - 1) * quarter), pl.ds(0, others * LANES)]
        wait_bytes(passed_on, b_ssem.at[k])
        wait_bytes(passed_on, b_rsem.at[k])

    first_to_xz()
    p_to_x()
    inner_to_z(0)
    gather(0, first_sum())
    p_to_z()
    inner_to_z(1)
    inner_to_core(0)
    solved = solve(0)

    inner_wait(0)
    update_to_x(0, apply_inner(0, solved))
    spread_z(0, reach[0])
    q_wait()
    inner_to_core(1)
    gather(1, q_recv[0] - update_sum(0))
    spread_y(0, reach[0])
    inner_wait(1)
    early = apply_inner(1, solved)
    solved = solve(1)

    update_to_x(1, early + apply_inner(2, solved))
    spread_z(1, reach[1])
    gather(2, q_recv[1] - update_sum(1))
    spread_y(1, reach[1])
    solve(2)
    spread_z(2, reach[2])
    spread_y(2, reach[2])

    spread_done(0, reach[0])
    spread_done(1, reach[1])
    wait_bytes(first_send.at[pl.ds(0, X * Z - 1)], first_ssem.at[0])
    wait_bytes(p_send.at[:, pl.ds(0, X - 1)], p_ssem.at[0])
    wait_bytes(q_send.at[:, pl.ds(0, Z - 1)], q_ssem.at[0])
    for slot in range(2):
        block = inner_v.at[steps[slot], pl.ds(1, Z - 1), my_half]
        wait_bytes(block, l_ssem.at[slot])
        wait_bytes(block, h_ssem.at[slot])
        wait_bytes(u_send.at[slot, pl.ds(0, X - 1)], u_ssem.at[slot])
    for k in range(3):
        gather_done(k)
    spread_done(2, reach[2])


def on_device(sizes, lower_prev, inner_blocks, diag_inverse, known_rows, right_sides):
    X, Y, Z = sizes
    step_rows = X * Y * Z * T
    f32 = jnp.float32
    dma = pltpu.SemaphoreType.DMA
    return pl.pallas_call(
        functools.partial(kernel, sizes),
        out_shape=pltpu.VMEM((3, step_rows // X, Z * LANES), f32),
        in_specs=[pl.BlockSpec(memory_space=pl.ANY)] * 5,
        out_specs=pl.BlockSpec(memory_space=pltpu.VMEM),
        scratch_shapes=[
            pltpu.VMEM(lower_prev.shape, f32),
            pltpu.VMEM(known_rows.shape, f32),
            pltpu.VMEM(diag_inverse.shape, f32),
            pltpu.VMEM(diag_inverse.shape, jnp.bfloat16),
            pltpu.VMEM(diag_inverse.shape, jnp.bfloat16),
            pltpu.VMEM(right_sides.shape, f32),
            pltpu.VMEM((3, Z) + inner_blocks.shape[1:], f32),
            pltpu.VMEM((X * Z, T, LANES), f32),
            pltpu.VMEM((X * Z, T, LANES), f32),
            pltpu.VMEM((2, X, T, Z * LANES), f32),
            pltpu.VMEM((2, X, T, Z * LANES), f32),
            pltpu.VMEM((2, Z, T, LANES), f32),
            pltpu.VMEM((2, Z, T, LANES), f32),
            pltpu.VMEM((3, Z, T, LANES), f32),
            pltpu.VMEM((3, Y, Z, X, T, LANES), f32),
            pltpu.VMEM((2, X, Z, T, LANES), f32),
            pltpu.VMEM((2, X, Z, T, LANES), f32),
            dma((4,)),
            dma((max(1, Z // 2),)),
            dma((1,)), dma((1,)),
            dma((1,)), dma((1,)),
            dma((1,)), dma((1,)),
            dma((2,)), dma((2,)),
            dma((2,)), dma((2,)),
            dma((2,)), dma((2,)),
            dma((3, X * Y)), dma((3, X * Y)),
            dma((3, Z)), dma((3, Z)),
            dma((3,)), dma((3,)),
        ],
        compiler_params=pltpu.CompilerParams(
            collective_id=0, has_side_effects=True, vmem_limit_bytes=56 * 1024 * 1024
        ),
    )(lower_prev, inner_blocks, diag_inverse, known_rows, right_sides)


def solution(mesh):
    X = mesh.shape["depth"]
    Y = 4 if mesh.shape["row"] == 32 else 2
    sizes = (X, Y, mesh.shape["row"] // Y)
    placed = (
        P(None, "row", "depth"),
        P(None, "row", "depth"),
        P(None, "depth", None),
        P("depth", "col"),
        P(None, "row", "col"),
    )
    return jax.shard_map(
        functools.partial(on_device, sizes),
        mesh=mesh,
        in_specs=placed,
        out_specs=P(None, "depth", "col"),
        check_vma=False,
    )
```

```python
import functools

import jax
import jax.numpy as jnp
from jax import lax
from jax.experimental import pallas as pl
from jax.experimental.pallas import tpu as pltpu
from jax.sharding import PartitionSpec as P

MESH = pl.DeviceIdType.MESH
T = 8
LANES = 128


def split(value):
    high = value.astype(jnp.bfloat16)
    low = (value - high.astype(jnp.float32)).astype(jnp.bfloat16)
    return high, low


def dot(a, b):
    return jnp.dot(a, b, preferred_element_type=jnp.float32)


def three_pass(a_high, a_low, b):
    b_high, b_low = split(b)
    width = b.shape[1]
    both = dot(a_high, jnp.concatenate([b_high, b_low], axis=1))
    return both[:, :width] + (both[:, width:] + dot(a_low, b_high))


def wrap(value, extent):
    return jnp.where(value >= extent, value - extent, value)


def wait_bytes(ref, sem):
    pltpu.make_async_copy(ref, ref, sem).wait()


def kernel(
    sizes,
    lower_hbm, inner_hbm, inverse_hbm, known_hbm, right_hbm,
    out_ref,
    lower_v, known_v, inverse_v, inverse_high, inverse_low, right_v, inner_v,
    first_send, first_recv, p_send, p_recv, q_send, q_recv, acc_v, red_v, product_v, u_send, u_recv,
    in_sem, known_sem,
    first_ssem, first_rsem, p_ssem, p_rsem, q_ssem, q_rsem, l_ssem, l_rsem, h_ssem, h_rsem, u_ssem, u_rsem, g_ssem, g_rsem,
    a_ssem, a_rsem, b_ssem, b_rsem,
):
    X, Y, Z = sizes
    reach = (1, 1, 2)
    row = lax.axis_index("row")
    col = lax.axis_index("col")
    x = lax.axis_index("depth")
    y = row // Z
    z = row % Z
    step_rows = X * Y * Z * T
    own = step_rows // X
    quarter = own // Y
    n_chunks = known_sem.shape[0]
    width = Z * LANES // n_chunks

    def on_x(o):
        return (row, col, wrap(x + o, X))

    def on_y(o):
        return (wrap(y + o, Y) * Z + z, col, x)

    def on_z(o):
        return (y * Z + wrap(z + o, Z), col, x)

    def z_lanes(pz):
        return pl.ds(pl.multiple_of(pz * LANES, LANES), LANES)

    def send(src, dst, ssem, rsem, device):
        pltpu.make_async_remote_copy(
            src, dst, ssem, rsem, device_id=device, device_id_type=MESH
        ).start()

    def far(o, extent):
        return min(o, extent - o)

    def far_first(extent):
        return sorted(range(1, extent), key=lambda o: -far(o, extent))

    xz = sorted(
        ((dx, dz) for dx in range(X) for dz in range(Z) if dx or dz),
        key=lambda d: -(far(d[0], X) + far(d[1], Z)),
    )
    xy = sorted(
        ((dx, dy) for dx in range(X) for dy in range(Y) if dx or dy),
        key=lambda d: -(far(d[0], X) + far(d[1], Y)),
    )

    lower_in = pltpu.make_async_copy(lower_hbm, lower_v, in_sem.at[0])
    lower_in.start()
    known_in = []
    for n in range(n_chunks):
        cut = pl.ds(n * width, width)
        copy = pltpu.make_async_copy(known_hbm.at[:, cut], known_v.at[:, cut], known_sem.at[n])
        copy.start()
        known_in.append(copy)
    right_in = pltpu.make_async_copy(right_hbm, right_v, in_sem.at[1])
    right_in.start()
    inner_in = pltpu.make_async_copy(inner_hbm, inner_v.at[:, 0], in_sem.at[2])
    inner_in.start()
    inverse_in = pltpu.make_async_copy(inverse_hbm, inverse_v, in_sem.at[3])
    inverse_in.start()

    barrier = pltpu.get_barrier_semaphore()
    for dx, dz in xz:
        device = (y * Z + wrap(z + dz, Z), col, wrap(x + dx, X))
        pl.semaphore_signal(barrier, inc=1, device_id=device, device_id_type=MESH)
    for o in range(1, Y):
        pl.semaphore_signal(barrier, inc=1, device_id=on_y(o), device_id_type=MESH)

    other_core = (row, 1 - col, x)
    pl.semaphore_signal(barrier, inc=1, device_id=other_core, device_id_type=MESH)

    for yy in range(1, Y):
        @pl.when(yy > x)
        def _():
            red_v[:, yy] = jnp.zeros_like(red_v[:, yy])

    lower_in.wait()
    right_in.wait()
    rows = 3 * X * T
    lower_high, lower_low = split(lower_v[...].reshape(rows, lower_v.shape[2]))
    lower_both = jnp.concatenate([lower_high, lower_low], axis=0)
    for n in range(n_chunks):
        known_in[n].wait()
        cut = slice(n * width, (n + 1) * width)
        k_high, k_low = split(known_v[:, cut])
        first = dot(lower_both, k_high)
        prod = first[:rows] + (first[rows:] + dot(lower_high, k_low))
        for k in range(3):
            for xd in range(X):
                base = (k * X + xd) * T
                mine = right_v[k, xd * T : (xd + 1) * T, cut]
                value = jnp.where(x == xd, mine, 0.0) - prod[base : base + T]
                if k > 0:
                    p_send[k - 1, xd, :, cut] = value
                else:
                    for zz in range(width // LANES):
                        zd = n * (width // LANES) + zz
                        first_send[xd * Z + zd] = value[:, zz * LANES : (zz + 1) * LANES]
    inverse_in.wait()
    for k in range(3):
        high, low = split(inverse_v[k])
        inverse_high[k] = high
        inverse_low[k] = low
    inner_in.wait()
    pl.semaphore_wait(barrier, len(xz) + Y)

    steps = (pl.ds(0, 1), pl.ds(1, 2))
    me = x * Z + z

    def first_to_xz():
        for dx, dz in xz:
            xd = wrap(x + dx, X)
            zd = wrap(z + dz, Z)
            send(
                first_send.at[xd * Z + zd], first_recv.at[me],
                first_ssem.at[0], first_rsem.at[0], (y * Z + zd, col, xd),
            )
        first_recv[me] = first_send[me]

    def first_sum():
        wait_bytes(first_recv.at[pl.ds(0, X * Z - 1)], first_rsem.at[0])
        total = first_recv[0:Z]
        for xs in range(1, X):
            total = total + first_recv[xs * Z : (xs + 1) * Z]
        return total

    def p_to_x():
        for o in far_first(X):
            there = wrap(x + o, X)
            send(p_send.at[:, there], p_recv.at[:, o], p_ssem.at[0], p_rsem.at[0], on_x(o))

    def p_to_z():
        wait_bytes(p_recv.at[:, pl.ds(1, X - 1)], p_rsem.at[0])
        for k in range(2):
            total = p_send[k, x]
            for o in range(1, X):
                total = total + p_recv[k, o]
            for zd in range(Z):
                q_send[k, zd] = total[:, zd * LANES : (zd + 1) * LANES]
            q_recv[k, z] = q_send[k, z]
        for o in far_first(Z):
            there = wrap(z + o, Z)
            send(q_send.at[:, there], q_recv.at[:, z], q_ssem.at[0], q_rsem.at[0], on_z(o))

    def q_wait():
        wait_bytes(q_recv.at[:, pl.ds(0, Z - 1)], q_rsem.at[0])

    half = X * T // 2
    my_half = pl.ds(pl.multiple_of(col * half, T), half)

    def inner_to_z(slot):
        for o in far_first(Z):
            send(
                inner_v.at[steps[slot], 0, my_half], inner_v.at[steps[slot], o, my_half],
                l_ssem.at[slot], l_rsem.at[slot], on_z(o),
            )

    def inner_to_core(slot):
        block = inner_v.at[steps[slot], pl.ds(1, Z - 1), my_half]
        wait_bytes(block, l_rsem.at[slot])
        send(block, block, h_ssem.at[slot], h_rsem.at[slot], other_core)

    def inner_wait(slot):
        wait_bytes(inner_v.at[steps[slot], pl.ds(1, Z - 1), my_half], h_rsem.at[slot])

    def gather(k, value):
        acc_v[k] = value
        red_v[k, y, :, x] = value
        for i, (dx, dy) in enumerate(xy):
            xd = wrap(x + dx, X)

            @pl.when(xd >= y)
            def _():
                send(
                    acc_v.at[k], red_v.at[k, y, :, x], g_ssem.at[k, i], g_rsem.at[k, i],
                    (wrap(y + dy, Y) * Z + z, col, xd),
                )

    def gather_done(k):
        for i, (dx, dy) in enumerate(xy):

            @pl.when(wrap(x + dx, X) >= y)
            def _():
                wait_bytes(acc_v.at[k], g_ssem.at[k, i])

    def solve(k):
        part = Z * X * T
        for dy in (0, *far_first(Y)[::-1]):
            ys = wrap(y + Y - dy, Y)
            for i, d in enumerate(xy):
                if d[1] == dy:

                    @pl.when(ys <= x)
                    def _():
                        xs = wrap(x + X - d[0], X)
                        wait_bytes(red_v.at[k, ys, :, xs], g_rsem.at[k, i])

            columns = pl.ds(pl.multiple_of(ys * part, part), part)
            product_v[ys] = three_pass(
                inverse_high[k, :, columns],
                inverse_low[k, :, columns],
                red_v[k, ys].reshape(part, LANES),
            )
        value = product_v[0]
        for ys in range(1, Y):
            value = value + product_v[ys]
        out_ref[k, :, z_lanes(z)] = value
        return value

    def apply_inner(which, value):
        high, low = split(inner_v[which].reshape(Z * X * T, inner_v.shape[3]))
        return three_pass(high, low, value).reshape(Z, X, T, LANES)

    def update_to_x(j, value):
        for o in range(Z):
            u_send[j, :, wrap(z + Z - o, Z)] = value[o]
        for o in far_first(X):
            there = wrap(x + o, X)
            send(u_send.at[j, there], u_recv.at[j, o], u_ssem.at[j], u_rsem.at[j], on_x(o))

    def update_sum(j):
        wait_bytes(u_recv.at[j, pl.ds(1, X - 1)], u_rsem.at[j])
        total = u_send[j, x]
        for o in range(1, X):
            total = total + u_recv[j, o]
        return total

    own_rows = pl.ds(pl.multiple_of(y * quarter, T), quarter)

    def spread_z(k, reach):
        block = out_ref.at[k, own_rows, z_lanes(z)]
        for o in far_first(Z):
            if far(o, Z) > reach:
                send(block, block, a_ssem.at[k, o], a_rsem.at[k, o], on_z(o))
        block = out_ref.at[k, :, z_lanes(z)]
        for o in far_first(Z)[::-1]:
            if far(o, Z) <= reach:
                send(block, block, a_ssem.at[k, o], a_rsem.at[k, o], on_z(o))

    def spread_y(k, reach):
        for o in far_first(Z)[::-1]:
            if far(o, Z) > reach:
                block = out_ref.at[k, own_rows, z_lanes(wrap(z + Z - o, Z))]
                wait_bytes(block, a_rsem.at[k, o])
                for p in far_first(Y):
                    send(block, block, b_ssem.at[k], b_rsem.at[k], on_y(p))

    def spread_done(k, reach):
        others = 0
        for o in range(1, Z):
            if far(o, Z) > reach:
                wait_bytes(out_ref.at[k, own_rows, z_lanes(z)], a_ssem.at[k, o])
                others += 1
            else:
                block = out_ref.at[k, :, z_lanes(z)]
                wait_bytes(block, a_ssem.at[k, o])
                wait_bytes(block, a_rsem.at[k, o])
        passed_on = out_ref.at[k, pl.ds(0, (Y - 1) * quarter), pl.ds(0, others * LANES)]
        wait_bytes(passed_on, b_ssem.at[k])
        wait_bytes(passed_on, b_rsem.at[k])

    first_to_xz()
    p_to_x()
    inner_to_z(0)
    gather(0, first_sum())
    p_to_z()
    inner_to_z(1)
    inner_to_core(0)
    solved = solve(0)

    inner_wait(0)
    update_to_x(0, apply_inner(0, solved))
    spread_z(0, reach[0])
    q_wait()
    inner_to_core(1)
    gather(1, q_recv[0] - update_sum(0))
    spread_y(0, reach[0])
    inner_wait(1)
    early = apply_inner(1, solved)
    solved = solve(1)

    update_to_x(1, early + apply_inner(2, solved))
    spread_z(1, reach[1])
    gather(2, q_recv[1] - update_sum(1))
    spread_y(1, reach[1])
    solve(2)
    spread_z(2, reach[2])
    spread_y(2, reach[2])

    spread_done(0, reach[0])
    spread_done(1, reach[1])
    wait_bytes(first_send.at[pl.ds(0, X * Z - 1)], first_ssem.at[0])
    wait_bytes(p_send.at[:, pl.ds(0, X - 1)], p_ssem.at[0])
    wait_bytes(q_send.at[:, pl.ds(0, Z - 1)], q_ssem.at[0])
    for slot in range(2):
        block = inner_v.at[steps[slot], pl.ds(1, Z - 1), my_half]
        wait_bytes(block, l_ssem.at[slot])
        wait_bytes(block, h_ssem.at[slot])
        wait_bytes(u_send.at[slot, pl.ds(0, X - 1)], u_ssem.at[slot])
    for k in range(3):
        gather_done(k)
    spread_done(2, reach[2])


def on_device(sizes, lower_prev, inner_blocks, diag_inverse, known_rows, right_sides):
    X, Y, Z = sizes
    step_rows = X * Y * Z * T
    f32 = jnp.float32
    dma = pltpu.SemaphoreType.DMA
    return pl.pallas_call(
        functools.partial(kernel, sizes),
        out_shape=pltpu.VMEM((3, step_rows // X, Z * LANES), f32),
        in_specs=[pl.BlockSpec(memory_space=pl.ANY)] * 5,
        out_specs=pl.BlockSpec(memory_space=pltpu.VMEM),
        scratch_shapes=[
            pltpu.VMEM(lower_prev.shape, f32),
            pltpu.VMEM(known_rows.shape, f32),
            pltpu.VMEM(diag_inverse.shape, f32),
            pltpu.VMEM(diag_inverse.shape, jnp.bfloat16),
            pltpu.VMEM(diag_inverse.shape, jnp.bfloat16),
            pltpu.VMEM(right_sides.shape, f32),
            pltpu.VMEM((3, Z) + inner_blocks.shape[1:], f32),
            pltpu.VMEM((X * Z, T, LANES), f32),
            pltpu.VMEM((X * Z, T, LANES), f32),
            pltpu.VMEM((2, X, T, Z * LANES), f32),
            pltpu.VMEM((2, X, T, Z * LANES), f32),
            pltpu.VMEM((2, Z, T, LANES), f32),
            pltpu.VMEM((2, Z, T, LANES), f32),
            pltpu.VMEM((3, Z, T, LANES), f32),
            pltpu.VMEM((3, Y, Z, X, T, LANES), f32),
            pltpu.VMEM((Y, step_rows // X, LANES), f32),
            pltpu.VMEM((2, X, Z, T, LANES), f32),
            pltpu.VMEM((2, X, Z, T, LANES), f32),
            dma((4,)),
            dma((max(1, Z // 2),)),
            dma((1,)), dma((1,)),
            dma((1,)), dma((1,)),
            dma((1,)), dma((1,)),
            dma((2,)), dma((2,)),
            dma((2,)), dma((2,)),
            dma((2,)), dma((2,)),
            dma((3, X * Y)), dma((3, X * Y)),
            dma((3, Z)), dma((3, Z)),
            dma((3,)), dma((3,)),
        ],
        compiler_params=pltpu.CompilerParams(
            collective_id=0, has_side_effects=True, vmem_limit_bytes=56 * 1024 * 1024
        ),
    )(lower_prev, inner_blocks, diag_inverse, known_rows, right_sides)


def solution(mesh):
    X = mesh.shape["depth"]
    Y = 4 if mesh.shape["row"] == 32 else 2
    sizes = (X, Y, mesh.shape["row"] // Y)
    placed = (
        P(None, "row", "depth"),
        P(None, "row", "depth"),
        P(None, "depth", None),
        P("depth", "col"),
        P(None, "row", "col"),
    )
    return jax.shard_map(
        functools.partial(on_device, sizes),
        mesh=mesh,
        in_specs=placed,
        out_specs=P(None, "depth", "col"),
        check_vma=False,
    )
```

```python
import functools

import jax
import jax.numpy as jnp
from jax import lax
from jax.experimental import pallas as pl
from jax.experimental.pallas import tpu as pltpu
from jax.sharding import PartitionSpec as P

MESH = pl.DeviceIdType.MESH
T = 8
LANES = 128


def split(value):
    high = value.astype(jnp.bfloat16)
    low = (value - high.astype(jnp.float32)).astype(jnp.bfloat16)
    return high, low


def dot(a, b):
    return jnp.dot(a, b, preferred_element_type=jnp.float32)


def three_pass(a_high, a_low, b):
    b_high, b_low = split(b)
    width = b.shape[1]
    both = dot(a_high, jnp.concatenate([b_high, b_low], axis=1))
    return both[:, :width] + (both[:, width:] + dot(a_low, b_high))


def wrap(value, extent):
    return jnp.where(value >= extent, value - extent, value)


def wait_bytes(ref, sem):
    pltpu.make_async_copy(ref, ref, sem).wait()


def kernel(
    sizes,
    lower_hbm, inner_hbm, inverse_hbm, known_hbm, right_hbm,
    out_ref,
    lower_v, known_v, inverse_v, inverse_high, inverse_low, right_v, inner_v,
    first_send, first_recv, p_send, p_recv, q_send, q_recv, acc_v, red_v, product_v, u_send, u_recv,
    in_sem, known_sem,
    first_ssem, first_rsem, p_ssem, p_rsem, q_ssem, q_rsem, l_ssem, l_rsem, h_ssem, h_rsem, u_ssem, u_rsem, g_ssem, g_rsem,
    a_ssem, a_rsem, b_ssem, b_rsem,
):
    X, Y, Z = sizes
    reach = (1, 1, 2)
    row = lax.axis_index("row")
    col = lax.axis_index("col")
    x = lax.axis_index("depth")
    y = row // Z
    z = row % Z
    step_rows = X * Y * Z * T
    own = step_rows // X
    quarter = own // Y
    n_chunks = known_sem.shape[0]
    width = Z * LANES // n_chunks

    def on_x(o):
        return (row, col, wrap(x + o, X))

    def on_y(o):
        return (wrap(y + o, Y) * Z + z, col, x)

    def on_z(o):
        return (y * Z + wrap(z + o, Z), col, x)

    def z_lanes(pz):
        return pl.ds(pl.multiple_of(pz * LANES, LANES), LANES)

    def send(src, dst, ssem, rsem, device):
        pltpu.make_async_remote_copy(
            src, dst, ssem, rsem, device_id=device, device_id_type=MESH
        ).start()

    def far(o, extent):
        return min(o, extent - o)

    def far_first(extent):
        return sorted(range(1, extent), key=lambda o: -far(o, extent))

    xz = sorted(
        ((dx, dz) for dx in range(X) for dz in range(Z) if dx or dz),
        key=lambda d: -(far(d[0], X) + far(d[1], Z)),
    )
    lower_in = pltpu.make_async_copy(lower_hbm, lower_v, in_sem.at[0])
    lower_in.start()
    known_in = []
    for n in range(n_chunks):
        cut = pl.ds(n * width, width)
        copy = pltpu.make_async_copy(known_hbm.at[:, cut], known_v.at[:, cut], known_sem.at[n])
        copy.start()
        known_in.append(copy)
    right_in = pltpu.make_async_copy(right_hbm, right_v, in_sem.at[1])
    right_in.start()
    inner_in = pltpu.make_async_copy(inner_hbm, inner_v.at[:, 0], in_sem.at[2])
    inner_in.start()
    inverse_in = pltpu.make_async_copy(inverse_hbm, inverse_v, in_sem.at[3])
    inverse_in.start()

    barrier = pltpu.get_barrier_semaphore()
    for dx, dz in xz:
        device = (y * Z + wrap(z + dz, Z), col, wrap(x + dx, X))
        pl.semaphore_signal(barrier, inc=1, device_id=device, device_id_type=MESH)
    for o in range(1, Y):
        pl.semaphore_signal(barrier, inc=1, device_id=on_y(o), device_id_type=MESH)

    other_core = (row, 1 - col, x)
    pl.semaphore_signal(barrier, inc=1, device_id=other_core, device_id_type=MESH)

    for yy in range(1, Y):
        @pl.when(yy > x)
        def _():
            red_v[:, yy] = jnp.zeros_like(red_v[:, yy])

    lower_in.wait()
    right_in.wait()
    rows = 3 * X * T
    lower_high, lower_low = split(lower_v[...].reshape(rows, lower_v.shape[2]))
    lower_both = jnp.concatenate([lower_high, lower_low], axis=0)
    for n in range(n_chunks):
        known_in[n].wait()
        cut = slice(n * width, (n + 1) * width)
        k_high, k_low = split(known_v[:, cut])
        first = dot(lower_both, k_high)
        prod = first[:rows] + (first[rows:] + dot(lower_high, k_low))
        for k in range(3):
            for xd in range(X):
                base = (k * X + xd) * T
                mine = right_v[k, xd * T : (xd + 1) * T, cut]
                value = jnp.where(x == xd, mine, 0.0) - prod[base : base + T]
                if k > 0:
                    p_send[k - 1, xd, :, cut] = value
                else:
                    for zz in range(width // LANES):
                        zd = n * (width // LANES) + zz
                        first_send[xd * Z + zd] = value[:, zz * LANES : (zz + 1) * LANES]
    inverse_in.wait()
    for k in range(3):
        high, low = split(inverse_v[k])
        inverse_high[k] = high
        inverse_low[k] = low
    inner_in.wait()
    pl.semaphore_wait(barrier, len(xz) + Y)

    steps = (pl.ds(0, 1), pl.ds(1, 2))
    me = x * Z + z

    def first_to_xz():
        for dx, dz in xz:
            xd = wrap(x + dx, X)
            zd = wrap(z + dz, Z)
            send(
                first_send.at[xd * Z + zd], first_recv.at[me],
                first_ssem.at[0], first_rsem.at[0], (y * Z + zd, col, xd),
            )
        first_recv[me] = first_send[me]

    def first_sum():
        wait_bytes(first_recv.at[pl.ds(0, X * Z - 1)], first_rsem.at[0])
        total = first_recv[0:Z]
        for xs in range(1, X):
            total = total + first_recv[xs * Z : (xs + 1) * Z]
        return total

    def p_to_x():
        for o in far_first(X):
            there = wrap(x + o, X)
            send(p_send.at[:, there], p_recv.at[:, o], p_ssem.at[0], p_rsem.at[0], on_x(o))

    def p_to_z():
        wait_bytes(p_recv.at[:, pl.ds(1, X - 1)], p_rsem.at[0])
        for k in range(2):
            total = p_send[k, x]
            for o in range(1, X):
                total = total + p_recv[k, o]
            for zd in range(Z):
                q_send[k, zd] = total[:, zd * LANES : (zd + 1) * LANES]
            q_recv[k, z] = q_send[k, z]
        for o in far_first(Z):
            there = wrap(z + o, Z)
            send(q_send.at[:, there], q_recv.at[:, z], q_ssem.at[0], q_rsem.at[0], on_z(o))

    def q_wait():
        wait_bytes(q_recv.at[:, pl.ds(0, Z - 1)], q_rsem.at[0])

    half = X * T // 2
    my_half = pl.ds(pl.multiple_of(col * half, T), half)

    def inner_to_z(slot):
        for o in far_first(Z):
            send(
                inner_v.at[steps[slot], 0, my_half], inner_v.at[steps[slot], o, my_half],
                l_ssem.at[slot], l_rsem.at[slot], on_z(o),
            )

    def inner_to_core(slot):
        block = inner_v.at[steps[slot], pl.ds(1, Z - 1), my_half]
        wait_bytes(block, l_rsem.at[slot])
        send(block, block, h_ssem.at[slot], h_rsem.at[slot], other_core)

    def inner_wait(slot):
        wait_bytes(inner_v.at[steps[slot], pl.ds(1, Z - 1), my_half], h_rsem.at[slot])

    order = [(xd, dy) for xd in range(X - 1, -1, -1) for dy in far_first(Y) + [0]]

    def sends(xd, dy):
        return (xd >= y) & (xd != x) if dy == 0 else xd >= y

    def gather(k, value):
        acc_v[k] = value
        red_v[k, y, :, x] = value
        for xd, dy in order:

            @pl.when(sends(xd, dy))
            def _():
                send(
                    acc_v.at[k], red_v.at[k, y, :, x],
                    g_ssem.at[k, xd * Y + dy], g_rsem.at[k, x * Y + dy],
                    (wrap(y + dy, Y) * Z + z, col, xd),
                )

    def gather_done(k):
        for xd, dy in order:

            @pl.when(sends(xd, dy))
            def _():
                wait_bytes(acc_v.at[k], g_ssem.at[k, xd * Y + dy])

    def solve(k):
        part = Z * X * T
        for dy in (0, *far_first(Y)[::-1]):
            ys = wrap(y + Y - dy, Y)
            for xs in range(X):

                @pl.when((ys <= x) & (xs != x) if dy == 0 else ys <= x)
                def _():
                    wait_bytes(red_v.at[k, ys, :, xs], g_rsem.at[k, xs * Y + dy])

            columns = pl.ds(pl.multiple_of(ys * part, part), part)
            product_v[ys] = three_pass(
                inverse_high[k, :, columns],
                inverse_low[k, :, columns],
                red_v[k, ys].reshape(part, LANES),
            )
        value = product_v[0]
        for ys in range(1, Y):
            value = value + product_v[ys]
        out_ref[k, :, z_lanes(z)] = value
        return value

    def apply_inner(which, value):
        high, low = split(inner_v[which].reshape(Z * X * T, inner_v.shape[3]))
        return three_pass(high, low, value).reshape(Z, X, T, LANES)

    def update_to_x(j, value):
        for o in range(Z):
            u_send[j, :, wrap(z + Z - o, Z)] = value[o]
        for o in far_first(X):
            there = wrap(x + o, X)
            send(u_send.at[j, there], u_recv.at[j, o], u_ssem.at[j], u_rsem.at[j], on_x(o))

    def update_sum(j):
        wait_bytes(u_recv.at[j, pl.ds(1, X - 1)], u_rsem.at[j])
        total = u_send[j, x]
        for o in range(1, X):
            total = total + u_recv[j, o]
        return total

    own_rows = pl.ds(pl.multiple_of(y * quarter, T), quarter)

    def spread_z(k, reach):
        block = out_ref.at[k, own_rows, z_lanes(z)]
        for o in far_first(Z):
            if far(o, Z) > reach:
                send(block, block, a_ssem.at[k, o], a_rsem.at[k, o], on_z(o))
        block = out_ref.at[k, :, z_lanes(z)]
        for o in far_first(Z)[::-1]:
            if far(o, Z) <= reach:
                send(block, block, a_ssem.at[k, o], a_rsem.at[k, o], on_z(o))

    def spread_y(k, reach):
        for o in far_first(Z)[::-1]:
            if far(o, Z) > reach:
                block = out_ref.at[k, own_rows, z_lanes(wrap(z + Z - o, Z))]
                wait_bytes(block, a_rsem.at[k, o])
                for p in far_first(Y):
                    send(block, block, b_ssem.at[k], b_rsem.at[k], on_y(p))

    def spread_done(k, reach):
        others = 0
        for o in range(1, Z):
            if far(o, Z) > reach:
                wait_bytes(out_ref.at[k, own_rows, z_lanes(z)], a_ssem.at[k, o])
                others += 1
            else:
                block = out_ref.at[k, :, z_lanes(z)]
                wait_bytes(block, a_ssem.at[k, o])
                wait_bytes(block, a_rsem.at[k, o])
        passed_on = out_ref.at[k, pl.ds(0, (Y - 1) * quarter), pl.ds(0, others * LANES)]
        wait_bytes(passed_on, b_ssem.at[k])
        wait_bytes(passed_on, b_rsem.at[k])

    first_to_xz()
    p_to_x()
    inner_to_z(0)
    gather(0, first_sum())
    p_to_z()
    inner_to_z(1)
    inner_to_core(0)
    solved = solve(0)

    inner_wait(0)
    update_to_x(0, apply_inner(0, solved))
    spread_z(0, reach[0])
    q_wait()
    inner_to_core(1)
    gather(1, q_recv[0] - update_sum(0))
    spread_y(0, reach[0])
    inner_wait(1)
    early = apply_inner(1, solved)
    solved = solve(1)

    update_to_x(1, early + apply_inner(2, solved))
    spread_z(1, reach[1])
    gather(2, q_recv[1] - update_sum(1))
    spread_y(1, reach[1])
    solve(2)
    spread_z(2, reach[2])
    spread_y(2, reach[2])

    spread_done(0, reach[0])
    spread_done(1, reach[1])
    wait_bytes(first_send.at[pl.ds(0, X * Z - 1)], first_ssem.at[0])
    wait_bytes(p_send.at[:, pl.ds(0, X - 1)], p_ssem.at[0])
    wait_bytes(q_send.at[:, pl.ds(0, Z - 1)], q_ssem.at[0])
    for slot in range(2):
        block = inner_v.at[steps[slot], pl.ds(1, Z - 1), my_half]
        wait_bytes(block, l_ssem.at[slot])
        wait_bytes(block, h_ssem.at[slot])
        wait_bytes(u_send.at[slot, pl.ds(0, X - 1)], u_ssem.at[slot])
    for k in range(3):
        gather_done(k)
    spread_done(2, reach[2])


def on_device(sizes, lower_prev, inner_blocks, diag_inverse, known_rows, right_sides):
    X, Y, Z = sizes
    step_rows = X * Y * Z * T
    f32 = jnp.float32
    dma = pltpu.SemaphoreType.DMA
    return pl.pallas_call(
        functools.partial(kernel, sizes),
        out_shape=pltpu.VMEM((3, step_rows // X, Z * LANES), f32),
        in_specs=[pl.BlockSpec(memory_space=pl.ANY)] * 5,
        out_specs=pl.BlockSpec(memory_space=pltpu.VMEM),
        scratch_shapes=[
            pltpu.VMEM(lower_prev.shape, f32),
            pltpu.VMEM(known_rows.shape, f32),
            pltpu.VMEM(diag_inverse.shape, f32),
            pltpu.VMEM(diag_inverse.shape, jnp.bfloat16),
            pltpu.VMEM(diag_inverse.shape, jnp.bfloat16),
            pltpu.VMEM(right_sides.shape, f32),
            pltpu.VMEM((3, Z) + inner_blocks.shape[1:], f32),
            pltpu.VMEM((X * Z, T, LANES), f32),
            pltpu.VMEM((X * Z, T, LANES), f32),
            pltpu.VMEM((2, X, T, Z * LANES), f32),
            pltpu.VMEM((2, X, T, Z * LANES), f32),
            pltpu.VMEM((2, Z, T, LANES), f32),
            pltpu.VMEM((2, Z, T, LANES), f32),
            pltpu.VMEM((3, Z, T, LANES), f32),
            pltpu.VMEM((3, Y, Z, X, T, LANES), f32),
            pltpu.VMEM((Y, step_rows // X, LANES), f32),
            pltpu.VMEM((2, X, Z, T, LANES), f32),
            pltpu.VMEM((2, X, Z, T, LANES), f32),
            dma((4,)),
            dma((max(1, Z // 2),)),
            dma((1,)), dma((1,)),
            dma((1,)), dma((1,)),
            dma((1,)), dma((1,)),
            dma((2,)), dma((2,)),
            dma((2,)), dma((2,)),
            dma((2,)), dma((2,)),
            dma((3, X * Y)), dma((3, X * Y)),
            dma((3, Z)), dma((3, Z)),
            dma((3,)), dma((3,)),
        ],
        compiler_params=pltpu.CompilerParams(
            collective_id=0, has_side_effects=True, vmem_limit_bytes=56 * 1024 * 1024
        ),
    )(lower_prev, inner_blocks, diag_inverse, known_rows, right_sides)


def solution(mesh):
    X = mesh.shape["depth"]
    Y = 4 if mesh.shape["row"] == 32 else 2
    sizes = (X, Y, mesh.shape["row"] // Y)
    placed = (
        P(None, "row", "depth"),
        P(None, "row", "depth"),
        P(None, "depth", None),
        P("depth", "col"),
        P(None, "row", "col"),
    )
    return jax.shard_map(
        functools.partial(on_device, sizes),
        mesh=mesh,
        in_specs=placed,
        out_specs=P(None, "depth", "col"),
        check_vma=False,
    )
```
